768 devices in a mesh: blk: 32 (over y_hi, x, core), grp: 24 (over z, y_lo).
Axes of the slice: x: 4, y: 8 (y_hi: 4, y_lo: 2; y = y_hi * 2 + y_lo), z: 12, core: 2. Of those that a mesh axis runs over, the one named last changes fastest.
Arguments:
- picture_embedding_array: bfloat16 [196608, 1152], P(('blk', 'grp')), may hold values from -0.1875 to 0.1875
- caption_embedding_array: bfloat16 [196608, 1152], P(('blk', 'grp')), may hold values from -0.1875 to 0.1875
- sharpness_multiplier: float32 [1], replicated, may hold values from 8 to 16
- score_offset: float32 [1], replicated, may hold values from -6 to -3
Outputs:
- row_loss: float32 [196608], P(('blk', 'grp'))
- grad_images: float32 [196608, 1152], P(('blk', 'grp'))
- grad_texts: float32 [196608, 1152], P(('blk', 'grp'))
The draws below stay inside these ranges and needn't reach their ends.
All inputs are finite; a program needn't handle non-finite values.
Results may differ from the reference program's by a relative error of at most 0.02.
Values may be sent and summed in bfloat16 or wider, within the bound.
No kernel may reach another device: no remote copies, remote signals or barrier semaphores. Data moves between devices by JAX's collectives and lax.ppermute only.
A program may use at most 32 MiB of HBM per device.

```python
import jax
import jax.numpy as jnp
from jax import lax

D = 1152
ROWS = 256
KSTEPS = 8
PAIRS = 196608


def shard_levels(key, extent, shards, smallest, high):
    loudness = 1.0
    for axis_at, blocks in shards:
        steps = jax.random.uniform(jax.random.fold_in(jax.random.fold_in(key, 6), axis_at), (blocks,), jnp.float32, smallest / len(shards), high / len(shards))
        loudness = loudness * jnp.repeat(jnp.exp(steps), extent[axis_at] // blocks).reshape((-1,) + (1,) * (len(extent) - 1 - axis_at))
    return loudness


def noise(key, dims, deviation, reach, split=(), kind=jnp.bfloat16):
    gain = shard_levels(key, dims, split, -0.22, 0.18) if split else 1.0
    result = jax.random.normal(key, dims, jnp.float32) * deviation * gain
    return jnp.minimum(jnp.maximum(result, -reach), reach).astype(kind)


def setup_inputs(seed: int = 0) -> dict:
    splits = jax.random.split(jax.random.key(seed), 5)
    return {
        "picture_embedding_array": noise(splits[0], (PAIRS, D), D ** -0.5, 0.1875, ((0, 768),)),
        "caption_embedding_array": noise(splits[1], (PAIRS, D), D ** -0.5, 0.1875, ((0, 768),)),
        "sharpness_multiplier": jnp.clip(jax.random.uniform(splits[2], (1,), jnp.float32, 8.0, 16.0), 8.0, 16.0),
        "score_offset": jnp.clip(jax.random.uniform(splits[3], (1,), jnp.float32, -6.0, -3.0), -6.0, -3.0),
    }


def normalize(raw):
    computed_quantities = raw.astype(jnp.float32)
    inverse = lax.rsqrt(lax.optimization_barrier(jnp.sum(computed_quantities * computed_quantities, axis=-1, keepdims=True)) + 1e-06)
    return (computed_quantities * inverse, inverse)

def unrounded_value(unit32):
    rounded = lax.optimization_barrier(unit32.astype(jnp.bfloat16))
    return rounded.astype(jnp.float32)

def back_norm(unit32, inverse, grad_unit):
    along = lax.optimization_barrier(jnp.sum(unit32 * grad_unit, axis=-1, keepdims=True))
    return inverse * (grad_unit - unit32 * along)

def reference(picture_embedding_array, caption_embedding_array, sharpness_multiplier, score_offset):
    smoothing_coefficient = sharpness_multiplier[0]
    block_displacement = score_offset[0]
    img_unit32, img_inverse = normalize(picture_embedding_array)
    txt_unit32, txt_inverse = normalize(caption_embedding_array)
    blocks = picture_embedding_array.shape[0] // ROWS
    image_unit_vectors = unrounded_value(img_unit32).reshape(blocks, ROWS, D)
    text_unit_vectors = unrounded_value(txt_unit32).reshape(blocks, ROWS, D)
    diagonal_mask = jnp.eye(ROWS, dtype=jnp.float32) > 0.5
    row_total_sum = jnp.zeros((blocks, ROWS), jnp.float32)
    grad_img = jnp.zeros((blocks, ROWS, D), jnp.float32)
    grad_txt = jnp.zeros((blocks, ROWS, D), jnp.float32)
    for hop_index in range(KSTEPS):
        rotated_blocks = jnp.roll(text_unit_vectors, hop_index, axis=0)
        pair_logit_matrix = smoothing_coefficient * jnp.einsum('clu,cxu->clx', image_unit_vectors, rotated_blocks) + block_displacement
        if hop_index == 0:
            target_labels = jnp.where(diagonal_mask, 1.0, -1.0).astype(jnp.float32)
        else:
            target_labels = jnp.full((ROWS, ROWS), -1.0, jnp.float32)
        row_total_sum = row_total_sum + lax.optimization_barrier(jnp.sum(jax.nn.softplus(-target_labels * pair_logit_matrix), axis=-1))
        sigmoid_weights = unrounded_value(-target_labels * jax.nn.sigmoid(-target_labels * pair_logit_matrix) * smoothing_coefficient)
        grad_img = grad_img + jnp.einsum('mrs,msd->mrd', sigmoid_weights, rotated_blocks)
        grad_txt = grad_txt + jnp.roll(jnp.einsum('mrs,mrd->msd', sigmoid_weights, image_unit_vectors), -hop_index, axis=0)
    grad_images = back_norm(img_unit32, img_inverse, grad_img.reshape(-1, D))
    grad_texts = back_norm(txt_unit32, txt_inverse, grad_txt.reshape(-1, D))
    return (row_total_sum.reshape(-1), grad_images, grad_texts)
```

```python
import functools

import jax
import jax.numpy as jnp
from jax import lax
from jax.experimental import pallas as pl
from jax.experimental.pallas import tpu as pltpu
from jax.sharding import PartitionSpec as P

AXES = ("blk", "grp")
BF16 = jnp.bfloat16
F32 = jnp.float32
EXTRA = 128


def vmem(count):
    return [pl.BlockSpec(memory_space=pltpu.VMEM)] * count


def smem(count):
    return [pl.BlockSpec(memory_space=pltpu.SMEM)] * count


def unit_and_inverse(raw):
    wide = raw.astype(F32)
    inverse = lax.rsqrt(jnp.sum(wide * wide, axis=-1, keepdims=True) + 1e-06)
    return wide * inverse, inverse


def prepare_kernel(flags, images, texts, x, y, both):
    rows = images.shape[0]
    img = unit_and_inverse(images[...])[0].astype(BF16)
    txt = unit_and_inverse(texts[...])[0].astype(BF16)
    even = flags[1] == 0

    @pl.when(even)
    def _():
        x[...] = txt
        both[:rows] = txt
        y[...] = img
        both[rows:] = img

    @pl.when(jnp.logical_not(even))
    def _():
        x[...] = img
        both[:rows] = img
        y[...] = txt
        both[rows:] = txt


def pair(scalars, rows, columns, diagonal):
    scale, offset = scalars[0], scalars[1]
    logits = (
        scale
        * lax.dot_general(rows, columns, (((1,), (1,)), ((), ())), preferred_element_type=F32)
        + offset
    )
    if diagonal:
        i = lax.broadcasted_iota(jnp.int32, logits.shape, 0)
        j = lax.broadcasted_iota(jnp.int32, logits.shape, 1)
        negated = jnp.where(i == j, -1.0, 1.0).astype(F32)
        logits = negated * logits
    small = jnp.exp(-jnp.abs(logits))
    share = 1.0 / (1.0 + small)
    sigmoid = jnp.where(logits >= 0, share, small * share)
    weights = sigmoid * scale
    if diagonal:
        weights = negated * weights
    loss = jnp.sum(jnp.maximum(logits, 0.0) + jnp.log1p(small), axis=-1, keepdims=True)
    return jnp.dot(weights.astype(BF16), columns, preferred_element_type=F32), loss


def early_kernel(
    flags, scalars, mine, other, x1, y1, x2, y2, acc_x, acc_y, loss_mine, loss_other
):
    rows = x1.shape[0]
    x_mine, y_mine = mine.at[:rows], mine.at[rows:]
    y_other, x_other = other.at[:rows], other.at[rows:]

    def side(own, own_columns, theirs, their_columns):
        total, loss = None, None
        for columns, diagonal in own_columns:
            grad, term = pair(scalars, own[...], columns[...], diagonal)
            total = grad if total is None else total + grad
            loss = term if loss is None else loss + term
        total_other, loss_other_ = None, None
        for columns in their_columns:
            grad, term = pair(scalars, theirs[...], columns[...], False)
            total_other = grad if total_other is None else total_other + grad
            loss_other_ = term if loss_other_ is None else loss_other_ + term
        return total, loss, total_other, loss_other_

    a, la, b, lb = side(x_mine, [(y_mine, True), (y1, False), (y2, False)], x_other, [y1, y2])
    acc_x[0] = a
    acc_x[1] = b
    a, lc, b, ld = side(
        y_mine, [(x_mine, True), (x1, False), (x2, False)], y_other, [x_mine, x1, x2]
    )
    acc_y[0] = a
    acc_y[1] = b
    images_are_y = flags[0] == 0
    loss_mine[...] = jnp.where(images_are_y, lc, la)
    loss_other[...] = jnp.where(images_are_y, ld, lb)


def y3_kernel(
    flags, scalars, mine, other, y3, acc_x, loss_mine, loss_other, new_x, new_mine, new_other
):
    rows = y3.shape[0]
    images_are_y = flags[0] == 0
    grad, loss = pair(scalars, mine[:rows], y3[...], False)
    new_x[0] = acc_x[0] + grad
    new_mine[...] = loss_mine[...] + jnp.where(images_are_y, 0.0, loss)
    grad, loss = pair(scalars, other[rows:], y3[...], False)
    new_x[1] = acc_x[1] + grad
    new_other[...] = loss_other[...] + jnp.where(images_are_y, 0.0, loss)


def with_loss(out, grad, loss):
    width = grad.shape[-1]
    out[:, :width] = grad.astype(BF16)
    high = loss.astype(BF16).astype(F32)
    lane = lax.broadcasted_iota(jnp.int32, (grad.shape[0], EXTRA), 1)
    out[:, width:] = jnp.where(lane < EXTRA // 2, high, loss - high).astype(BF16)


def loss_in(block, width):
    high = block[:, width : width + 1].astype(F32)
    low = block[:, width + EXTRA // 2 : width + EXTRA // 2 + 1].astype(F32)
    return high + low


def x3_kernel(
    flags, scalars, mine, other, x3, acc_y, loss_mine, loss_other, out_y, new_mine, new_other, send
):
    rows = x3.shape[0]
    images_are_y = flags[0] == 0
    grad, loss = pair(scalars, other[:rows], x3[...], False)
    total_other = loss_other[...] + jnp.where(images_are_y, loss, 0.0)
    new_other[...] = total_other
    with_loss(send, acc_y[1] + grad, total_other)
    grad, loss = pair(scalars, mine[rows:], x3[...], False)
    out_y[...] = acc_y[0] + grad
    new_mine[...] = loss_mine[...] + jnp.where(images_are_y, loss, 0.0)


def y4_kernel(flags, scalars, other, y4, acc_x, loss_other, send):
    rows = y4.shape[0]
    images_are_y = flags[0] == 0
    grad, loss = pair(scalars, other[rows:], y4[...], False)
    with_loss(send, acc_x[1] + grad, loss_other[...] + jnp.where(images_are_y, 0.0, loss))


def sum_kernel(at, acc, loss, received, send):
    width = acc.shape[-1]
    own = acc[...] if at is None else acc[at]
    block = received[...]
    with_loss(
        send,
        own + block[:, :width].astype(F32),
        loss[...] + loss_in(block, width),
    )


def finish_kernel(
    flags,
    images,
    texts,
    acc_x,
    acc_y,
    loss_mine,
    from_core_x,
    from_core_y,
    home_x,
    home_y,
    loss_out,
    grad_images,
    grad_texts,
):
    width = images.shape[-1]
    stays = flags[0] == flags[1]
    images_are_x = flags[1] == 1

    def write(out, raw, grad):
        unit, inverse = unit_and_inverse(raw[...])
        along = jnp.sum(unit * grad, axis=-1, keepdims=True)
        out[...] = inverse * (grad - unit * along)

    def write_both(grad_x, loss_x, grad_y, loss_y):
        @pl.when(images_are_x)
        def _():
            write(grad_images, images, grad_x())
            write(grad_texts, texts, grad_y())
            loss_out[...] = loss_x()

        @pl.when(jnp.logical_not(images_are_x))
        def _():
            write(grad_images, images, grad_y())
            write(grad_texts, texts, grad_x())
            loss_out[...] = loss_y()

    @pl.when(stays)
    def _():
        write_both(
            lambda: acc_x[0] + from_core_x[:, :width].astype(F32),
            lambda: loss_mine[...] + loss_in(from_core_x, width),
            lambda: acc_y[...] + from_core_y[:, :width].astype(F32),
            lambda: loss_mine[...] + loss_in(from_core_y, width),
        )

    @pl.when(jnp.logical_not(stays))
    def _():
        write_both(
            lambda: home_x[:, :width].astype(F32),
            lambda: loss_in(home_x, width),
            lambda: home_y[:, :width].astype(F32),
            lambda: loss_in(home_y, width),
        )


def call(kernel, outs, n_smem, args):
    return pl.pallas_call(
        kernel,
        out_shape=outs,
        in_specs=smem(n_smem) + vmem(len(args) - n_smem),
        out_specs=vmem(len(outs)),
        compiler_params=pltpu.CompilerParams(vmem_limit_bytes=48 * 1024 * 1024),
        cost_estimate=pl.CostEstimate(flops=1, bytes_accessed=1, transcendentals=0),
    )(*args)


def tied(block, *earlier):
    return lax.optimization_barrier((block, *earlier))[0]


def routes(blks, grps):
    total = blks * grps

    def turned(device):
        blk, grp = divmod(device, grps)
        return (blk - blk % 2 + grp % 2) * grps + grp - grp % 2 + blk % 2

    def step(block, role):
        texts = (block % 2 == 0) == (role == "x")
        return (block + (2 if texts else -2)) % total

    blocks = range(total)
    first = {r: [(b, turned(step(b, r))) for b in blocks] for r in "xy"}
    later = {r: [(turned(b), turned(step(b, r))) for b in blocks] for r in "xy"}
    swap = [(b, turned(b)) for b in blocks]
    home = [(turned(b), b) for b in blocks if turned(b) != b]

    def across(device):
        blk, grp = divmod(device, grps)
        return (blk + 1 - 2 * (blk % 2)) * grps + grp

    cores = [(b, across(b)) for b in blocks]
    return first, later, swap, home, cores


def on_device(images, texts, scale, offset):
    rows, width = images.shape
    blks, grps = lax.axis_size("blk"), lax.axis_size("grp")
    first, later, swap, home, cores = routes(blks, grps)
    flags = jnp.stack([lax.axis_index("blk") % 2, lax.axis_index("grp") % 2]).astype(jnp.int32)
    scalars = jnp.concatenate([scale, offset])
    move = lambda block, route: lax.ppermute(block, AXES, route)

    block = jax.ShapeDtypeStruct((rows, width), BF16)
    wide = jax.ShapeDtypeStruct((rows, width + EXTRA), BF16)
    column = jax.ShapeDtypeStruct((rows, 1), F32)
    total = jax.ShapeDtypeStruct((rows, width), F32)
    totals = jax.ShapeDtypeStruct((2, rows, width), F32)
    work = 4 * rows * rows * width

    x, y, both = call(
        prepare_kernel,
        (block, block, jax.ShapeDtypeStruct((2 * rows, width), BF16)),
        1,
        (flags, images, texts),
    )
    y1 = move(y, first["y"])
    x1 = move(x, first["x"])
    y2 = move(y1, later["y"])
    x2 = move(x1, later["x"])
    mine = move(tied(both, x1, y1), swap)
    other = move(tied(mine, x2, y2), cores)
    y3 = move(y2, later["y"])
    x3 = move(x2, later["x"])

    acc_x, acc_y, loss_mine, loss_other = call(
        early_kernel,
        (totals, totals, column, column),
        2,
        (flags, scalars, mine, other, x1, y1, x2, y2),
    )
    y3 = tied(y3, acc_x)
    y4 = move(y3, later["y"])
    acc_x, loss_mine, loss_other = call(
        y3_kernel,
        (totals, column, column),
        2,
        (flags, scalars, mine, other, y3, acc_x, loss_mine, loss_other),
    )
    x3 = tied(x3, acc_x)
    acc_y, loss_mine, loss_other, send_y = call(
        x3_kernel,
        (total, column, column, wide),
        2,
        (flags, scalars, mine, other, x3, acc_y, loss_mine, loss_other),
    )
    from_core_x = move(send_y, cores)
    (back_x,) = call(
        functools.partial(sum_kernel, 0), (wide,), 0, (acc_x, loss_mine, from_core_x)
    )
    home_x = move(back_x, home)
    y4 = tied(y4, back_x)
    (send_x,) = call(
        y4_kernel,
        (wide,),
        2,
        (flags, scalars, other, y4, acc_x, loss_other),
    )
    from_core_y = move(send_x, cores)
    (back_y,) = call(
        functools.partial(sum_kernel, None), (wide,), 0, (acc_y, loss_mine, from_core_y)
    )
    home_y = move(back_y, home)
    loss, grad_images, grad_texts = call(
        finish_kernel,
        (column, total, total),
        1,
        (
            flags,
            images,
            texts,
            acc_x,
            acc_y,
            loss_mine,
            from_core_x,
            from_core_y,
            home_x,
            home_y,
        ),
    )
    return loss.reshape(rows), grad_images, grad_texts


def solution(mesh):
    return jax.shard_map(
        on_device,
        mesh=mesh,
        in_specs=(P(AXES, None), P(AXES, None), P(), P()),
        out_specs=(P(AXES), P(AXES, None), P(AXES, None)),
        check_vma=False,
    )
```

```python
import functools

import jax
import jax.numpy as jnp
from jax import lax
from jax.experimental import pallas as pl
from jax.experimental.pallas import tpu as pltpu
from jax.sharding import PartitionSpec as P

AXES = ("blk", "grp")
BF16 = jnp.bfloat16
F32 = jnp.float32
EXTRA = 128
PIECES = 4
LAST = 288


def vmem(count):
    return [pl.BlockSpec(memory_space=pltpu.VMEM)] * count


def smem(count):
    return [pl.BlockSpec(memory_space=pltpu.SMEM)] * count


def unit_and_inverse(raw):
    wide = raw.astype(F32)
    inverse = lax.rsqrt(jnp.sum(wide * wide, axis=-1, keepdims=True) + 1e-06)
    return wide * inverse, inverse


def prepare_kernel(flags, images, texts, both):
    rows = images.shape[0]
    img = unit_and_inverse(images[...])[0].astype(BF16)
    txt = unit_and_inverse(texts[...])[0].astype(BF16)
    even = flags[1] == 0

    @pl.when(even)
    def _():
        both[:rows] = txt
        both[rows:] = img

    @pl.when(jnp.logical_not(even))
    def _():
        both[:rows] = img
        both[rows:] = txt


def stack_kernel(second, first, stacked):
    rows = first.shape[0]
    stacked[:rows] = unit_and_inverse(first[...])[0].astype(BF16)
    stacked[rows:] = unit_and_inverse(second[...])[0].astype(BF16)


def joined(a, b):
    return a + b + a * b


def pair(scalars, rows, columns, diagonal=False):
    scale, offset = scalars[0], scalars[1]
    logits = (
        scale
        * lax.dot_general(rows, columns, (((1,), (1,)), ((), ())), preferred_element_type=F32)
        + offset
    )
    if diagonal:
        i = lax.broadcasted_iota(jnp.int32, logits.shape, 0)
        j = lax.broadcasted_iota(jnp.int32, logits.shape, 1)
        negated = jnp.where(i == j, -1.0, 1.0).astype(F32)
        logits = negated * logits
    small = jnp.exp(-jnp.abs(logits))
    share = scale / (1.0 + small)
    weights = jnp.where(logits >= 0, share, small * share)
    if diagonal:
        weights = negated * weights
    above = jnp.maximum(logits, 0.0)
    half = logits.shape[1] // 2
    return (
        jnp.dot(weights.astype(BF16), columns, preferred_element_type=F32),
        above[:, :half] + above[:, half:],
        joined(small[:, :half], small[:, half:]),
    )


def side(scalars, rows, columns):
    total = None
    for block, diagonal in columns:
        grad, above, small = pair(scalars, rows, block[...], diagonal)
        if total is None:
            total, total_above, total_small = grad, above, small
        else:
            total = total + grad
            total_above = total_above + above
            total_small = joined(total_small, small)
    return total, total_above, total_small


def early_kernel(scalars, mine, other, pair1, pair2, acc, above, small):
    rows = mine.shape[0] // 2
    later = [(c.at[at : at + rows], False) for c in (pair1, pair2) for at in (0, rows)]
    first, second = (other.at[rows:], True), (mine.at[:rows], True)
    acc[0], above[0], small[0] = side(
        scalars, other[:rows], [first, (mine.at[:rows], False)] + later
    )
    acc[1], above[1], small[1] = side(scalars, mine[rows:], [second] + later)


def with_loss(out, grad, loss):
    width = grad.shape[-1]
    out[:, :width] = grad.astype(BF16)
    high = loss.astype(BF16).astype(F32)
    lane = lax.broadcasted_iota(jnp.int32, (grad.shape[0], EXTRA), 1)
    out[:, width:] = jnp.where(lane < EXTRA // 2, high, loss - high).astype(BF16)


def loss_of(above, small):
    return jnp.sum(above + jnp.log1p(small), axis=-1, keepdims=True)


def loss_in(block, width):
    high = block[:, width : width + 1].astype(F32)
    low = block[:, width + EXTRA // 2 : width + EXTRA // 2 + 1].astype(F32)
    return high + low


def third_first_kernel(scalars, other, pair3, acc, above, small, send):
    rows = other.shape[0] // 2
    grad, more_above, more_small = side(
        scalars, other[:rows], [(pair3.at[:rows], False), (pair3.at[rows:], False)]
    )
    with_loss(send, acc[0] + grad, loss_of(above[0] + more_above, joined(small[0], more_small)))


def third_second_kernel(scalars, mine, pair3, acc, above, small, new_acc, new_above, new_small):
    rows = mine.shape[0] // 2
    grad, more_above, more_small = side(
        scalars, mine[rows:], [(pair3.at[:rows], False), (pair3.at[rows:], False)]
    )
    new_acc[...] = acc[1] + grad
    new_above[...] = above[1] + more_above
    new_small[...] = joined(small[1], more_small)


def fourth_kernel(scalars, mine, last, acc, above, small, send):
    rows = mine.shape[0] // 2
    grad, more_above, more_small = side(scalars, mine[rows:], [(last.at[:rows], False)])
    with_loss(
        send, acc[...] + grad, loss_of(above[...] + more_above, joined(small[...], more_small))
    )


def as_row(column):
    count = column.shape[0]
    i = lax.broadcasted_iota(jnp.int32, (count, count), 0)
    j = lax.broadcasted_iota(jnp.int32, (count, count), 1)
    return jnp.sum(jnp.where(i == j, column, 0.0), axis=0, keepdims=True)


def back_norm(raw, grad):
    unit, inverse = unit_and_inverse(raw)
    along = jnp.sum(unit * grad, axis=-1, keepdims=True)
    return inverse * (grad - unit * along)


def write_grad(is_image, images, texts, block, grad_images, grad_texts, buf, sem):
    rows, width = images.shape
    count = rows // PIECES

    def copies(out):
        return [
            pltpu.make_async_copy(
                buf.at[at * count : (at + 1) * count],
                out.at[at * count : (at + 1) * count],
                sem.at[at],
            )
            for at in range(PIECES)
        ]

    def write(raw, out):
        for at, copy in enumerate(copies(out)):
            part = slice(at * count, (at + 1) * count)
            buf[part] = back_norm(raw[part], block[part, :width].astype(F32))
            copy.start()
        for copy in copies(out):
            copy.wait()

    pl.when(is_image)(lambda: write(images, grad_images))
    pl.when(jnp.logical_not(is_image))(lambda: write(texts, grad_texts))


def finish_first_kernel(flags, images, texts, block, grad_images, grad_texts, loss, buf, sem):
    loss[...] = as_row(loss_in(block, images.shape[1]))
    write_grad(flags[1] == 1, images, texts, block, grad_images, grad_texts, buf, sem)


def finish_second_kernel(
    flags,
    images,
    texts,
    block,
    loss_first,
    images_so_far,
    texts_so_far,
    grad_images,
    grad_texts,
    loss,
    buf,
    sem,
):
    loss[...] = jnp.where(
        flags[1] == 1, loss_first[...], as_row(loss_in(block, images.shape[1]))
    )
    write_grad(flags[1] == 0, images, texts, block, grad_images, grad_texts, buf, sem)


def call(kernel, outs, n_smem, args, in_hbm=0, outs_hbm=0, scratch=(), aliases=None, us=0.0):
    hbm = lambda count: [pl.BlockSpec(memory_space=pl.ANY)] * count
    return pl.pallas_call(
        kernel,
        out_shape=outs,
        in_specs=smem(n_smem) + vmem(len(args) - n_smem - in_hbm) + hbm(in_hbm),
        out_specs=tuple(hbm(outs_hbm) + vmem(len(outs) - outs_hbm)),
        scratch_shapes=list(scratch),
        input_output_aliases=aliases or {},
        compiler_params=pltpu.CompilerParams(vmem_limit_bytes=24 * 1024 * 1024),
        cost_estimate=pl.CostEstimate(
            flops=1, bytes_accessed=1 + int(us * 3.7e6), transcendentals=0
        ),
    )(*args)


def tied(block, *earlier):
    return lax.optimization_barrier((block, *earlier))[0]


def routes(blks, grps):
    total = blks * grps

    def held_at(block):
        blk, grp = divmod(block, grps)
        turns = blk // 2 % 4 != 3
        column = (blk + (turns and grp >= grps // 2)) % 2
        return blk - blk % 2, grp - grp % 2 + column

    def on_core(block, core):
        blk, grp = held_at(block)
        return (blk + core) * grps + grp

    blocks = range(total)
    ahead = lambda b: (b + 2) % total
    behind = lambda b: (b - 2) % total
    even = [b for b in blocks if b % 2 == 0]
    odd = [b for b in blocks if b % 2 == 1]
    first_x = [(b, on_core(ahead(b), 0)) for b in even] + [(b, on_core(behind(b), 1)) for b in odd]
    first_y = [(b, on_core(behind(b), 1)) for b in even] + [(b, on_core(ahead(b), 0)) for b in odd]
    later = [(on_core(b, 0), on_core(ahead(b), 0)) for b in even]
    later += [(on_core(b, 1), on_core(behind(b), 1)) for b in even]
    swap = [(b, on_core(b, b % 2)) for b in blocks]
    cores = [(on_core(b, b % 2), on_core(b, 1 - b % 2)) for b in blocks]
    home_first = [(on_core(b, 0), b) for b in odd] + [(on_core(b, 1), b) for b in even]
    home_second = [(on_core(b, 0), b) for b in even] + [(on_core(b, 1), b) for b in odd]
    return first_x, first_y, later, swap, cores, home_first, home_second


def on_device(images, texts, scale, offset):
    rows, width = images.shape
    blks, grps = lax.axis_size("blk"), lax.axis_size("grp")
    first_x, first_y, later, swap, cores, home_first, home_second = routes(blks, grps)
    flags = jnp.stack([lax.axis_index("blk") % 2, lax.axis_index("grp") % 2]).astype(jnp.int32)
    scalars = jnp.concatenate([scale, offset])
    move = lambda block, route: lax.ppermute(block, AXES, route)

    double = jax.ShapeDtypeStruct((2 * rows, width), BF16)
    wide = jax.ShapeDtypeStruct((rows, width + EXTRA), BF16)
    row = jax.ShapeDtypeStruct((1, rows), F32)
    term = jax.ShapeDtypeStruct((rows, rows // 2), F32)
    terms = jax.ShapeDtypeStruct((2, rows, rows // 2), F32)
    total = jax.ShapeDtypeStruct((rows, width), F32)
    totals = jax.ShapeDtypeStruct((2, rows, width), F32)
    scratch = (pltpu.VMEM((rows, width), F32), pltpu.SemaphoreType.DMA((PIECES,)))

    even = lax.axis_index("grp") % 2 == 0
    x1 = move(jnp.where(even, texts, images), first_x)
    y1 = move(jnp.where(even, images, texts), first_y)
    (both,) = call(prepare_kernel, (double,), 1, (flags, images, texts))
    (pair1,) = call(stack_kernel, (double,), 0, (x1, y1))
    pair2 = move(pair1, later)
    mine = move(both, swap)
    pair3 = move(pair2, later)
    other = move(mine, cores)

    acc, above, small = call(
        early_kernel, (totals, terms, terms), 1, (scalars, mine, other, pair1, pair2)
    )
    pair3 = tied(pair3, acc)
    last = move(pair3[:LAST], later)
    (send_first,) = call(
        third_first_kernel, (wide,), 1, (scalars, other, pair3, acc, above, small)
    )
    back_first = move(send_first, home_first)
    acc, above, small = call(
        third_second_kernel,
        (total, term, term),
        1,
        (scalars, mine, tied(pair3, send_first), acc, above, small),
    )
    (send_second,) = call(
        fourth_kernel, (wide,), 1, (scalars, mine, tied(last, back_first), acc, above, small)
    )
    back_second = move(send_second, home_second)
    grad_images, grad_texts, loss = call(
        finish_first_kernel,
        (total, total, row),
        1,
        (flags, images, texts, tied(back_first, send_second)),
        outs_hbm=2,
        scratch=scratch,
    )
    grad_images, grad_texts, loss = call(
        finish_second_kernel,
        (total, total, row),
        1,
        (flags, images, texts, tied(back_second, loss), loss, grad_images, grad_texts),
        in_hbm=2,
        outs_hbm=2,
        scratch=scratch,
        aliases={5: 0, 6: 1},
    )
    return loss.reshape(rows), grad_images, grad_texts


def solution(mesh):
    return jax.shard_map(
        on_device,
        mesh=mesh,
        in_specs=(P(AXES, None), P(AXES, None), P(), P()),
        out_specs=(P(AXES), P(AXES, None), P(AXES, None)),
        check_vma=False,
    )
```

```python
import functools

import jax
import jax.numpy as jnp
from jax import lax
from jax.experimental import pallas as pl
from jax.experimental.pallas import tpu as pltpu
from jax.sharding import PartitionSpec as P

AXES = ("blk", "grp")
BF16 = jnp.bfloat16
F32 = jnp.float32
EXTRA = 128
PIECES = 4
SPARE = 32


def vmem(count):
    return [pl.BlockSpec(memory_space=pltpu.VMEM)] * count


def smem(count):
    return [pl.BlockSpec(memory_space=pltpu.SMEM)] * count


def unit_and_inverse(raw):
    wide = raw.astype(F32)
    inverse = lax.rsqrt(jnp.sum(wide * wide, axis=-1, keepdims=True) + 1e-06)
    return wide * inverse, inverse


def prepare_kernel(flags, images, texts, x, y, both):
    rows = images.shape[0]
    img = unit_and_inverse(images[...])[0].astype(BF16)
    txt = unit_and_inverse(texts[...])[0].astype(BF16)

    def write(first, second):
        x[...] = first
        both[:rows] = first
        y[...] = second
        both[rows:] = second

    pl.when(flags[1] == 0)(lambda: write(txt, img))
    pl.when(flags[1] == 1)(lambda: write(img, txt))


def joined(a, b):
    return a + b + a * b


def pair(scalars, rows, columns, diagonal=False):
    scale, offset = scalars[0], scalars[1]
    logits = (
        scale
        * lax.dot_general(rows, columns, (((1,), (1,)), ((), ())), preferred_element_type=F32)
        + offset
    )
    if diagonal:
        i = lax.broadcasted_iota(jnp.int32, logits.shape, 0)
        j = lax.broadcasted_iota(jnp.int32, logits.shape, 1)
        negated = jnp.where(i == j, -1.0, 1.0).astype(F32)
        logits = negated * logits
    small = jnp.exp(-jnp.abs(logits))
    share = scale / (1.0 + small)
    weights = jnp.where(logits >= 0, share, small * share)
    if diagonal:
        weights = negated * weights
    above = jnp.maximum(logits, 0.0)
    half = logits.shape[1] // 2
    return (
        jnp.dot(weights.astype(BF16), columns, preferred_element_type=F32),
        above[:, :half] + above[:, half:],
        joined(small[:, :half], small[:, half:]),
    )


def side(scalars, rows, columns):
    total = None
    for block, diagonal in columns:
        grad, above, small = pair(scalars, rows, block[...], diagonal)
        if total is None:
            total, total_above, total_small = grad, above, small
        else:
            total = total + grad
            total_above = total_above + above
            total_small = joined(total_small, small)
    return total, total_above, total_small


def whole(halves):
    return jnp.concatenate([half[...] for half in halves], axis=0)


def early_kernel(scalars, mine, low, middle, a1, b1, a2, b2, acc, above, small):
    rows = a1.shape[0]
    other = whole((low, middle))
    other_x, other_y = other[:rows], other[rows:]
    later = [(block, False) for block in (a1, b1, a2, b2)]
    acc[0], above[0], small[0] = side(
        scalars, other_x, [(other_y, True), (mine.at[:rows], False)] + later
    )
    acc[1], above[1], small[1] = side(scalars, mine[rows:], [(mine.at[:rows], True)] + later)


def with_loss(out, grad, loss):
    width = grad.shape[-1]
    out[:, :width] = grad.astype(BF16)
    high = loss.astype(BF16).astype(F32)
    lane = lax.broadcasted_iota(jnp.int32, (grad.shape[0], EXTRA), 1)
    out[:, width:] = jnp.where(lane < EXTRA // 2, high, loss - high).astype(BF16)


def loss_of(above, small):
    return jnp.sum(above + jnp.log1p(small), axis=-1, keepdims=True)


def loss_in(block, width):
    high = block[:, width : width + 1].astype(F32)
    low = block[:, width + EXTRA // 2 : width + EXTRA // 2 + 1].astype(F32)
    return high + low


def third_first_kernel(scalars, low, middle, a3, b3, acc, above, small, send):
    grad, more_above, more_small = side(scalars, whole((low, middle))[: a3.shape[0]], [(a3, False), (b3, False)])
    with_loss(send, acc[0] + grad, loss_of(above[0] + more_above, joined(small[0], more_small)))


def third_second_kernel(scalars, mine, a3, b3, acc, above, small, new_acc, new_above, new_small):
    rows = a3.shape[0]
    grad, more_above, more_small = side(scalars, mine[rows:], [(a3, False), (b3, False)])
    new_acc[...] = acc[1] + grad
    new_above[...] = above[1] + more_above
    new_small[...] = joined(small[1], more_small)


def fourth_kernel(scalars, mine, a4, acc, above, small, send):
    rows = mine.shape[0] // 2
    grad, more_above, more_small = side(scalars, mine[rows:], [(a4.at[:rows], False)])
    with_loss(
        send, acc[...] + grad, loss_of(above[...] + more_above, joined(small[...], more_small))
    )


def as_row(column):
    count = column.shape[0]
    i = lax.broadcasted_iota(jnp.int32, (count, count), 0)
    j = lax.broadcasted_iota(jnp.int32, (count, count), 1)
    return jnp.sum(jnp.where(i == j, column, 0.0), axis=0, keepdims=True)


def back_norm(raw, grad):
    unit, inverse = unit_and_inverse(raw)
    along = jnp.sum(unit * grad, axis=-1, keepdims=True)
    return inverse * (grad - unit * along)


def write_grad(is_image, images, texts, block, grad_images, grad_texts, buf, sem):
    rows, width = images.shape
    count = rows // PIECES

    def copies(out):
        return [
            pltpu.make_async_copy(
                buf.at[at * count : (at + 1) * count],
                out.at[at * count : (at + 1) * count],
                sem.at[at],
            )
            for at in range(PIECES)
        ]

    def write(raw, out):
        for at, copy in enumerate(copies(out)):
            part = slice(at * count, (at + 1) * count)
            buf[part] = back_norm(raw[part], block[part, :width].astype(F32))
            copy.start()
        for copy in copies(out):
            copy.wait()

    pl.when(is_image)(lambda: write(images, grad_images))
    pl.when(jnp.logical_not(is_image))(lambda: write(texts, grad_texts))


def finish_first_kernel(flags, images, texts, block, grad_images, grad_texts, loss, buf, sem):
    loss[...] = as_row(loss_in(block, images.shape[1]))
    write_grad(flags[1] == 1, images, texts, block, grad_images, grad_texts, buf, sem)


def finish_second_kernel(
    flags,
    images,
    texts,
    block,
    loss_first,
    images_so_far,
    texts_so_far,
    grad_images,
    grad_texts,
    loss,
    buf,
    sem,
):
    loss[...] = jnp.where(
        flags[1] == 1, loss_first[...], as_row(loss_in(block, images.shape[1]))
    )
    write_grad(flags[1] == 0, images, texts, block, grad_images, grad_texts, buf, sem)


def call(kernel, outs, n_smem, args, in_hbm=0, outs_hbm=0, scratch=(), aliases=None, us=0.0):
    hbm = lambda count: [pl.BlockSpec(memory_space=pl.ANY)] * count
    return pl.pallas_call(
        kernel,
        out_shape=outs,
        in_specs=smem(n_smem) + vmem(len(args) - n_smem - in_hbm) + hbm(in_hbm),
        out_specs=tuple(hbm(outs_hbm) + vmem(len(outs) - outs_hbm)),
        scratch_shapes=list(scratch),
        input_output_aliases=aliases or {},
        compiler_params=pltpu.CompilerParams(vmem_limit_bytes=24 * 1024 * 1024),
        cost_estimate=pl.CostEstimate(
            flops=1, bytes_accessed=1 + int(us * 3.7e6), transcendentals=0
        ),
    )(*args)


def tied(block, *earlier):
    return lax.optimization_barrier((block, *earlier))[0]


def routes(blks, grps):
    total = blks * grps

    def held_at(block):
        blk, grp = divmod(block, grps)
        turns = blk // 2 % 4 != 3
        column = (blk + (turns and grp >= grps // 2)) % 2
        return blk - blk % 2, grp - grp % 2 + column

    def on_core(block, core):
        blk, grp = held_at(block)
        return (blk + core) * grps + grp

    blocks = range(total)
    ahead = lambda b: (b + 2) % total
    behind = lambda b: (b - 2) % total
    even = [b for b in blocks if b % 2 == 0]
    odd = [b for b in blocks if b % 2 == 1]
    first_x = [(b, on_core(ahead(b), 0)) for b in even] + [(b, on_core(behind(b), 1)) for b in odd]
    first_y = [(b, on_core(behind(b), 1)) for b in even] + [(b, on_core(ahead(b), 0)) for b in odd]
    later = [(on_core(b, 0), on_core(ahead(b), 0)) for b in even]
    later += [(on_core(b, 1), on_core(behind(b), 1)) for b in even]
    swap = [(b, on_core(b, b % 2)) for b in blocks]
    cores = [(on_core(b, b % 2), on_core(b, 1 - b % 2)) for b in blocks]
    home_first = [(on_core(b, 0), b) for b in odd] + [(on_core(b, 1), b) for b in even]
    home_second = [(on_core(b, 0), b) for b in even] + [(on_core(b, 1), b) for b in odd]
    return first_x, first_y, later, swap, cores, home_first, home_second


def on_device(images, texts, scale, offset):
    rows, width = images.shape
    blks, grps = lax.axis_size("blk"), lax.axis_size("grp")
    first_x, first_y, later, swap, cores, home_first, home_second = routes(blks, grps)
    flags = jnp.stack([lax.axis_index("blk") % 2, lax.axis_index("grp") % 2]).astype(jnp.int32)
    scalars = jnp.concatenate([scale, offset])
    move = lambda block, route: lax.ppermute(block, AXES, route)

    double = jax.ShapeDtypeStruct((2 * rows, width), BF16)
    wide = jax.ShapeDtypeStruct((rows, width + EXTRA), BF16)
    row = jax.ShapeDtypeStruct((1, rows), F32)
    term = jax.ShapeDtypeStruct((rows, rows // 2), F32)
    terms = jax.ShapeDtypeStruct((2, rows, rows // 2), F32)
    total = jax.ShapeDtypeStruct((rows, width), F32)
    totals = jax.ShapeDtypeStruct((2, rows, width), F32)
    scratch = (pltpu.VMEM((rows, width), F32), pltpu.SemaphoreType.DMA((PIECES,)))

    block = jax.ShapeDtypeStruct((rows, width), BF16)
    x, y, both = call(prepare_kernel, (block, block, double), 1, (flags, images, texts))
    b1, a1 = move(x, first_x), move(y, first_y)
    b2, a2 = move(b1, later), move(a1, later)
    b3, a3 = move(b2, later), move(a2, later)
    mine = move(both, swap)
    step = rows
    other = [move(mine[at : at + step], cores) for at in range(0, 2 * rows, step)]

    acc, above, small = call(
        early_kernel,
        (totals, terms, terms),
        1,
        (scalars, tied(mine, a3), *other, a1, b1, a2, b2),
    )
    a4 = move(jnp.concatenate([a3, a2[:SPARE]]), later)
    (send_first,) = call(
        third_first_kernel, (wide,), 1, (scalars, *other[:2], a3, b3, acc, above, small)
    )
    back_first = move(send_first, home_first)
    acc, above, small = call(
        third_second_kernel,
        (total, term, term),
        1,
        (scalars, mine, tied(a3, send_first), b3, acc, above, small),
    )
    (send_second,) = call(fourth_kernel, (wide,), 1, (scalars, mine, a4, acc, above, small))
    send_second = tied(send_second, back_first)
    back_second = move(send_second, home_second)
    grad_images, grad_texts, loss = call(
        finish_first_kernel,
        (total, total, row),
        1,
        (flags, images, texts, tied(back_first, send_second)),
        outs_hbm=2,
        scratch=scratch,
    )
    grad_images, grad_texts, loss = call(
        finish_second_kernel,
        (total, total, row),
        1,
        (flags, images, texts, tied(back_second, loss), loss, grad_images, grad_texts),
        in_hbm=2,
        outs_hbm=2,
        scratch=scratch,
        aliases={5: 0, 6: 1},
    )
    return loss.reshape(rows), grad_images, grad_texts


def solution(mesh):
    return jax.shard_map(
        on_device,
        mesh=mesh,
        in_specs=(P(AXES, None), P(AXES, None), P(), P()),
        out_specs=(P(AXES), P(AXES, None), P(AXES, None)),
        check_vma=False,
    )
```

```python
import functools

import jax
import jax.numpy as jnp
from jax import lax
from jax.experimental import pallas as pl
from jax.experimental.pallas import tpu as pltpu
from jax.sharding import PartitionSpec as P

AXES = ("blk", "grp")
BF16 = jnp.bfloat16
F32 = jnp.float32
EXTRA = 128
PIECES = 4
SPARE = 32


def vmem(count):
    return [pl.BlockSpec(memory_space=pltpu.VMEM)] * count


def smem(count):
    return [pl.BlockSpec(memory_space=pltpu.SMEM)] * count


def unit_and_inverse(raw):
    wide = raw.astype(F32)
    inverse = lax.rsqrt(jnp.sum(wide * wide, axis=-1, keepdims=True) + 1e-06)
    return wide * inverse, inverse


def prepare_kernel(flags, images, texts, x, y, both):
    rows = images.shape[0]
    img = unit_and_inverse(images[...])[0].astype(BF16)
    txt = unit_and_inverse(texts[...])[0].astype(BF16)

    def write(first, second):
        x[...] = first
        both[:rows] = first
        y[...] = second
        both[rows:] = second

    pl.when(flags[1] == 0)(lambda: write(txt, img))
    pl.when(flags[1] == 1)(lambda: write(img, txt))


def joined(a, b):
    return a + b + a * b


def pair(scalars, rows, columns, diagonal=False):
    scale, offset = scalars[0], scalars[1]
    logits = (
        scale
        * lax.dot_general(rows, columns, (((1,), (1,)), ((), ())), preferred_element_type=F32)
        + offset
    )
    if diagonal:
        i = lax.broadcasted_iota(jnp.int32, logits.shape, 0)
        j = lax.broadcasted_iota(jnp.int32, logits.shape, 1)
        negated = jnp.where(i == j, -1.0, 1.0).astype(F32)
        logits = negated * logits
    small = jnp.exp(-jnp.abs(logits))
    share = scale / (1.0 + small)
    weights = jnp.where(logits >= 0, share, small * share)
    if diagonal:
        weights = negated * weights
    above = jnp.maximum(logits, 0.0)
    half = logits.shape[1] // 2
    return (
        jnp.dot(weights.astype(BF16), columns, preferred_element_type=F32),
        above[:, :half] + above[:, half:],
        joined(small[:, :half], small[:, half:]),
    )


def side(scalars, rows, columns):
    total = None
    for block, diagonal in columns:
        grad, above, small = pair(scalars, rows, block[...], diagonal)
        if total is None:
            total, total_above, total_small = grad, above, small
        else:
            total = total + grad
            total_above = total_above + above
            total_small = joined(total_small, small)
    return total, total_above, total_small


def whole(halves):
    return jnp.concatenate([half[...] for half in halves], axis=0)


def early_kernel(scalars, mine, low, middle, a1, b1, a2, b2, acc, above, small):
    rows = a1.shape[0]
    other = whole((low, middle))
    other_x, other_y = other[:rows], other[rows:]
    later = [(block, False) for block in (a1, b1, a2, b2)]
    acc[0], above[0], small[0] = side(
        scalars, other_x, [(other_y, True), (mine.at[:rows], False)] + later
    )
    acc[1], above[1], small[1] = side(scalars, mine[rows:], [(mine.at[:rows], True)] + later)


def with_loss(out, grad, loss):
    width = grad.shape[-1]
    out[:, :width] = grad.astype(BF16)
    high = loss.astype(BF16).astype(F32)
    lane = lax.broadcasted_iota(jnp.int32, (grad.shape[0], EXTRA), 1)
    out[:, width:] = jnp.where(lane < EXTRA // 2, high, loss - high).astype(BF16)


def loss_of(above, small):
    return jnp.sum(above + jnp.log1p(small), axis=-1, keepdims=True)


def loss_in(block, width):
    high = block[:, width : width + 1].astype(F32)
    low = block[:, width + EXTRA // 2 : width + EXTRA // 2 + 1].astype(F32)
    return high + low


def third_first_kernel(scalars, low, middle, a3, b3, acc, above, small, send):
    grad, more_above, more_small = side(scalars, whole((low, middle))[: a3.shape[0]], [(a3, False), (b3, False)])
    with_loss(send, acc[0] + grad, loss_of(above[0] + more_above, joined(small[0], more_small)))


def third_second_kernel(scalars, mine, a3, b3, acc, above, small, new_acc, new_above, new_small):
    rows = a3.shape[0]
    grad, more_above, more_small = side(scalars, mine[rows:], [(a3, False), (b3, False)])
    new_acc[...] = acc[1] + grad
    new_above[...] = above[1] + more_above
    new_small[...] = joined(small[1], more_small)


def fourth_kernel(scalars, mine, a4, acc, above, small, send):
    rows = mine.shape[0] // 2
    grad, more_above, more_small = side(scalars, mine[rows:], [(a4.at[:rows], False)])
    with_loss(
        send, acc[...] + grad, loss_of(above[...] + more_above, joined(small[...], more_small))
    )


def as_row(column):
    count = column.shape[0]
    i = lax.broadcasted_iota(jnp.int32, (count, count), 0)
    j = lax.broadcasted_iota(jnp.int32, (count, count), 1)
    return jnp.sum(jnp.where(i == j, column, 0.0), axis=0, keepdims=True)


def back_norm(raw, grad):
    unit, inverse = unit_and_inverse(raw)
    along = jnp.sum(unit * grad, axis=-1, keepdims=True)
    return inverse * (grad - unit * along)


def write_grad(is_image, images, texts, block, grad_images, grad_texts, buf, sem):
    rows, width = images.shape
    count = rows // PIECES

    def copies(out):
        return [
            pltpu.make_async_copy(
                buf.at[at * count : (at + 1) * count],
                out.at[at * count : (at + 1) * count],
                sem.at[at],
            )
            for at in range(PIECES)
        ]

    def write(raw, out):
        for at, copy in enumerate(copies(out)):
            part = slice(at * count, (at + 1) * count)
            buf[part] = back_norm(raw[part], block[part, :width].astype(F32))
            copy.start()
        for copy in copies(out):
            copy.wait()

    pl.when(is_image)(lambda: write(images, grad_images))
    pl.when(jnp.logical_not(is_image))(lambda: write(texts, grad_texts))


def finish_first_kernel(flags, images, texts, block, grad_images, grad_texts, loss, buf, sem):
    loss[...] = as_row(loss_in(block, images.shape[1]))
    write_grad(flags[1] == 1, images, texts, block, grad_images, grad_texts, buf, sem)


def finish_second_kernel(
    flags,
    images,
    texts,
    block,
    loss_first,
    images_so_far,
    texts_so_far,
    grad_images,
    grad_texts,
    loss,
    buf,
    sem,
):
    loss[...] = jnp.where(
        flags[1] == 1, loss_first[...], as_row(loss_in(block, images.shape[1]))
    )
    write_grad(flags[1] == 0, images, texts, block, grad_images, grad_texts, buf, sem)


def call(kernel, outs, n_smem, args, in_hbm=0, outs_hbm=0, scratch=(), aliases=None, us=0.0):
    hbm = lambda count: [pl.BlockSpec(memory_space=pl.ANY)] * count
    return pl.pallas_call(
        kernel,
        out_shape=outs,
        in_specs=smem(n_smem) + vmem(len(args) - n_smem - in_hbm) + hbm(in_hbm),
        out_specs=tuple(hbm(outs_hbm) + vmem(len(outs) - outs_hbm)),
        scratch_shapes=list(scratch),
        input_output_aliases=aliases or {},
        compiler_params=pltpu.CompilerParams(vmem_limit_bytes=24 * 1024 * 1024),
        cost_estimate=pl.CostEstimate(
            flops=1, bytes_accessed=1 + int(us * 3.7e6), transcendentals=0
        ),
    )(*args)


def tied(block, *earlier):
    return lax.optimization_barrier((block, *earlier))[0]


def routes(blks, grps):
    total = blks * grps

    def held_at(block):
        blk, grp = divmod(block, grps)
        across = blk // 2 % 4
        turns = across != 1
        column = (blk + (across > 1) + (turns and grp >= grps // 2)) % 2
        return blk - blk % 2, grp - grp % 2 + column

    def on_core(block, core):
        blk, grp = held_at(block)
        return (blk + core) * grps + grp

    blocks = range(total)
    ahead = lambda b: (b + 2) % total
    behind = lambda b: (b - 2) % total
    even = [b for b in blocks if b % 2 == 0]
    odd = [b for b in blocks if b % 2 == 1]
    first_x = [(b, on_core(ahead(b), 0)) for b in even] + [(b, on_core(behind(b), 1)) for b in odd]
    first_y = [(b, on_core(behind(b), 1)) for b in even] + [(b, on_core(ahead(b), 0)) for b in odd]
    later = [(on_core(b, 0), on_core(ahead(b), 0)) for b in even]
    later += [(on_core(b, 1), on_core(behind(b), 1)) for b in even]
    swap = [(b, on_core(b, b % 2)) for b in blocks]
    cores = [(on_core(b, b % 2), on_core(b, 1 - b % 2)) for b in blocks]
    home_first = [(on_core(b, 0), b) for b in odd] + [(on_core(b, 1), b) for b in even]
    home_second = [(on_core(b, 0), b) for b in even] + [(on_core(b, 1), b) for b in odd]
    return first_x, first_y, later, swap, cores, home_first, home_second


def on_device(images, texts, scale, offset):
    rows, width = images.shape
    blks, grps = lax.axis_size("blk"), lax.axis_size("grp")
    first_x, first_y, later, swap, cores, home_first, home_second = routes(blks, grps)
    flags = jnp.stack([lax.axis_index("blk") % 2, lax.axis_index("grp") % 2]).astype(jnp.int32)
    scalars = jnp.concatenate([scale, offset])
    move = lambda block, route: lax.ppermute(block, AXES, route)

    double = jax.ShapeDtypeStruct((2 * rows, width), BF16)
    wide = jax.ShapeDtypeStruct((rows, width + EXTRA), BF16)
    row = jax.ShapeDtypeStruct((1, rows), F32)
    term = jax.ShapeDtypeStruct((rows, rows // 2), F32)
    terms = jax.ShapeDtypeStruct((2, rows, rows // 2), F32)
    total = jax.ShapeDtypeStruct((rows, width), F32)
    totals = jax.ShapeDtypeStruct((2, rows, width), F32)
    scratch = (pltpu.VMEM((rows, width), F32), pltpu.SemaphoreType.DMA((PIECES,)))

    block = jax.ShapeDtypeStruct((rows, width), BF16)
    x, y, both = call(prepare_kernel, (block, block, double), 1, (flags, images, texts))
    b1, a1 = move(x, first_x), move(y, first_y)
    b2, a2 = move(b1, later), move(a1, later)
    b3, a3 = move(b2, later), move(a2, later)
    mine = move(both, swap)
    step = rows
    other = [move(mine[at : at + step], cores) for at in range(0, 2 * rows, step)]

    acc, above, small = call(
        early_kernel,
        (totals, terms, terms),
        1,
        (scalars, tied(mine, a3), *other, a1, b1, a2, b2),
    )
    a4 = move(jnp.concatenate([a3, a2[:SPARE]]), later)
    (send_first,) = call(
        third_first_kernel, (wide,), 1, (scalars, *other[:2], a3, b3, acc, above, small)
    )
    back_first = move(send_first, home_first)
    acc, above, small = call(
        third_second_kernel,
        (total, term, term),
        1,
        (scalars, mine, tied(a3, send_first), b3, acc, above, small),
    )
    (send_second,) = call(fourth_kernel, (wide,), 1, (scalars, mine, a4, acc, above, small))
    send_second = tied(send_second, back_first)
    back_second = move(send_second, home_second)
    grad_images, grad_texts, loss = call(
        finish_first_kernel,
        (total, total, row),
        1,
        (flags, images, texts, tied(back_first, send_second)),
        outs_hbm=2,
        scratch=scratch,
    )
    grad_images, grad_texts, loss = call(
        finish_second_kernel,
        (total, total, row),
        1,
        (flags, images, texts, tied(back_second, loss), loss, grad_images, grad_texts),
        in_hbm=2,
        outs_hbm=2,
        scratch=scratch,
        aliases={5: 0, 6: 1},
    )
    return loss.reshape(rows), grad_images, grad_texts


def solution(mesh):
    return jax.shard_map(
        on_device,
        mesh=mesh,
        in_specs=(P(AXES, None), P(AXES, None), P(), P()),
        out_specs=(P(AXES), P(AXES, None), P(AXES, None)),
        check_vma=False,
    )
```

```python
import functools

import jax
import jax.numpy as jnp
from jax import lax
from jax.experimental import pallas as pl
from jax.experimental.pallas import tpu as pltpu
from jax.sharding import PartitionSpec as P

AXES = ("blk", "grp")
BF16 = jnp.bfloat16
F32 = jnp.float32
EXTRA = 128
PIECES = 4
SPARE = 32


def vmem(count):
    return [pl.BlockSpec(memory_space=pltpu.VMEM)] * count


def smem(count):
    return [pl.BlockSpec(memory_space=pltpu.SMEM)] * count


def unit_and_inverse(raw):
    wide = raw.astype(F32)
    inverse = lax.rsqrt(jnp.sum(wide * wide, axis=-1, keepdims=True) + 1e-06)
    return wide * inverse, inverse


def prepare_kernel(flags, images, texts, x, y, both):
    rows = images.shape[0]
    img = unit_and_inverse(images[...])[0].astype(BF16)
    txt = unit_and_inverse(texts[...])[0].astype(BF16)

    def write(first, second):
        x[...] = first
        both[:rows] = first
        y[...] = second
        both[rows:] = second

    pl.when(flags[1] == 0)(lambda: write(txt, img))
    pl.when(flags[1] == 1)(lambda: write(img, txt))


def joined(a, b):
    return a + b + a * b


def pair(scalars, rows, columns, diagonal=False):
    scale, offset = scalars[0], scalars[1]
    logits = (
        scale
        * lax.dot_general(rows, columns, (((1,), (1,)), ((), ())), preferred_element_type=F32)
        + offset
    )
    if diagonal:
        i = lax.broadcasted_iota(jnp.int32, logits.shape, 0)
        j = lax.broadcasted_iota(jnp.int32, logits.shape, 1)
        negated = jnp.where(i == j, -1.0, 1.0).astype(F32)
        logits = negated * logits
    small = jnp.exp(-jnp.abs(logits))
    share = scale / (1.0 + small)
    weights = jnp.where(logits >= 0, share, small * share)
    if diagonal:
        weights = negated * weights
    above = jnp.maximum(logits, 0.0)
    half = logits.shape[1] // 2
    return (
        jnp.dot(weights.astype(BF16), columns, preferred_element_type=F32),
        above[:, :half] + above[:, half:],
        joined(small[:, :half], small[:, half:]),
    )


def side(scalars, rows, columns):
    total = None
    for block, diagonal in columns:
        grad, above, small = pair(scalars, rows, block[...], diagonal)
        if total is None:
            total, total_above, total_small = grad, above, small
        else:
            total = total + grad
            total_above = total_above + above
            total_small = joined(total_small, small)
    return total, total_above, total_small


def whole(halves):
    return jnp.concatenate([half[...] for half in halves], axis=0)


def early_kernel(scalars, mine, low, middle, a1, b1, a2, b2, acc, above, small):
    rows = a1.shape[0]
    other = whole((low, middle))
    other_x, other_y = other[:rows], other[rows:]
    later = [(block, False) for block in (a1, b1, a2, b2)]
    acc[0], above[0], small[0] = side(
        scalars, other_x, [(other_y, True), (mine.at[:rows], False)] + later
    )
    acc[1], above[1], small[1] = side(scalars, mine[rows:], [(mine.at[:rows], True)] + later)


def with_loss(out, grad, loss):
    width = grad.shape[-1]
    out[:, :width] = grad.astype(BF16)
    high = loss.astype(BF16).astype(F32)
    lane = lax.broadcasted_iota(jnp.int32, (grad.shape[0], EXTRA), 1)
    out[:, width:] = jnp.where(lane < EXTRA // 2, high, loss - high).astype(BF16)


def loss_of(above, small):
    return jnp.sum(above + jnp.log1p(small), axis=-1, keepdims=True)


def loss_in(block, width):
    high = block[:, width : width + 1].astype(F32)
    low = block[:, width + EXTRA // 2 : width + EXTRA // 2 + 1].astype(F32)
    return high + low


def third_first_kernel(scalars, low, middle, a3, b3, acc, above, small, send):
    grad, more_above, more_small = side(scalars, whole((low, middle))[: a3.shape[0]], [(a3, False), (b3, False)])
    with_loss(send, acc[0] + grad, loss_of(above[0] + more_above, joined(small[0], more_small)))


def third_second_kernel(scalars, mine, a3, b3, acc, above, small, new_acc, new_above, new_small):
    rows = a3.shape[0]
    grad, more_above, more_small = side(scalars, mine[rows:], [(a3, False), (b3, False)])
    new_acc[...] = acc[1] + grad
    new_above[...] = above[1] + more_above
    new_small[...] = joined(small[1], more_small)


def fourth_kernel(scalars, mine, a4, acc, above, small, send):
    rows = mine.shape[0] // 2
    grad, more_above, more_small = side(scalars, mine[rows:], [(a4.at[:rows], False)])
    with_loss(
        send, acc[...] + grad, loss_of(above[...] + more_above, joined(small[...], more_small))
    )


def as_row(column):
    count = column.shape[0]
    i = lax.broadcasted_iota(jnp.int32, (count, count), 0)
    j = lax.broadcasted_iota(jnp.int32, (count, count), 1)
    return jnp.sum(jnp.where(i == j, column, 0.0), axis=0, keepdims=True)


def back_norm(raw, grad):
    unit, inverse = unit_and_inverse(raw)
    along = jnp.sum(unit * grad, axis=-1, keepdims=True)
    return inverse * (grad - unit * along)


def write_grad(is_image, images, texts, block, grad_images, grad_texts, buf, sem, meanwhile):
    rows, width = images.shape
    count = rows // PIECES

    def copies(out):
        return [
            pltpu.make_async_copy(
                buf.at[at * count : (at + 1) * count],
                out.at[at * count : (at + 1) * count],
                sem.at[at],
            )
            for at in range(PIECES)
        ]

    def write(raw, out):
        for at, copy in enumerate(copies(out)):
            part = slice(at * count, (at + 1) * count)
            buf[part] = back_norm(raw[part], block[part, :width].astype(F32))
            copy.start()
        meanwhile()
        for copy in copies(out):
            copy.wait()

    pl.when(is_image)(lambda: write(images, grad_images))
    pl.when(jnp.logical_not(is_image))(lambda: write(texts, grad_texts))


def finish_first_kernel(flags, images, texts, block, grad_images, grad_texts, loss, buf, sem):
    def write_loss():
        loss[...] = as_row(loss_in(block, images.shape[1]))

    write_grad(flags[1] == 1, images, texts, block, grad_images, grad_texts, buf, sem, write_loss)


def finish_second_kernel(
    flags,
    images,
    texts,
    block,
    loss_first,
    images_so_far,
    texts_so_far,
    grad_images,
    grad_texts,
    loss,
    buf,
    sem,
):
    def write_loss():
        loss[...] = jnp.where(
            flags[1] == 1, loss_first[...], as_row(loss_in(block, images.shape[1]))
        )

    write_grad(flags[1] == 0, images, texts, block, grad_images, grad_texts, buf, sem, write_loss)


def call(kernel, outs, n_smem, args, in_hbm=0, outs_hbm=0, scratch=(), aliases=None, us=0.0):
    hbm = lambda count: [pl.BlockSpec(memory_space=pl.ANY)] * count
    return pl.pallas_call(
        kernel,
        out_shape=outs,
        in_specs=smem(n_smem) + vmem(len(args) - n_smem - in_hbm) + hbm(in_hbm),
        out_specs=tuple(hbm(outs_hbm) + vmem(len(outs) - outs_hbm)),
        scratch_shapes=list(scratch),
        input_output_aliases=aliases or {},
        compiler_params=pltpu.CompilerParams(vmem_limit_bytes=24 * 1024 * 1024),
        cost_estimate=pl.CostEstimate(
            flops=1, bytes_accessed=1 + int(us * 3.7e6), transcendentals=0
        ),
    )(*args)


def tied(block, *earlier):
    return lax.optimization_barrier((block, *earlier))[0]


def routes(blks, grps):
    total = blks * grps

    def held_at(block):
        blk, grp = divmod(block, grps)
        across = blk // 2 % 4
        turns = across != 1
        column = (blk + (across > 1) + (turns and grp >= grps // 2)) % 2
        return blk - blk % 2, grp - grp % 2 + column

    def on_core(block, core):
        blk, grp = held_at(block)
        return (blk + core) * grps + grp

    blocks = range(total)
    ahead = lambda b: (b + 2) % total
    behind = lambda b: (b - 2) % total
    even = [b for b in blocks if b % 2 == 0]
    odd = [b for b in blocks if b % 2 == 1]
    first_x = [(b, on_core(ahead(b), 0)) for b in even] + [(b, on_core(behind(b), 1)) for b in odd]
    first_y = [(b, on_core(behind(b), 1)) for b in even] + [(b, on_core(ahead(b), 0)) for b in odd]
    later = [(on_core(b, 0), on_core(ahead(b), 0)) for b in even]
    later += [(on_core(b, 1), on_core(behind(b), 1)) for b in even]
    swap = [(b, on_core(b, b % 2)) for b in blocks]
    cores = [(on_core(b, b % 2), on_core(b, 1 - b % 2)) for b in blocks]
    home_first = [(on_core(b, 0), b) for b in odd] + [(on_core(b, 1), b) for b in even]
    home_second = [(on_core(b, 0), b) for b in even] + [(on_core(b, 1), b) for b in odd]
    return first_x, first_y, later, swap, cores, home_first, home_second


def on_device(images, texts, scale, offset):
    rows, width = images.shape
    blks, grps = lax.axis_size("blk"), lax.axis_size("grp")
    first_x, first_y, later, swap, cores, home_first, home_second = routes(blks, grps)
    flags = jnp.stack([lax.axis_index("blk") % 2, lax.axis_index("grp") % 2]).astype(jnp.int32)
    scalars = jnp.concatenate([scale, offset])
    move = lambda block, route: lax.ppermute(block, AXES, route)

    double = jax.ShapeDtypeStruct((2 * rows, width), BF16)
    wide = jax.ShapeDtypeStruct((rows, width + EXTRA), BF16)
    row = jax.ShapeDtypeStruct((1, rows), F32)
    term = jax.ShapeDtypeStruct((rows, rows // 2), F32)
    terms = jax.ShapeDtypeStruct((2, rows, rows // 2), F32)
    total = jax.ShapeDtypeStruct((rows, width), F32)
    totals = jax.ShapeDtypeStruct((2, rows, width), F32)
    scratch = (pltpu.VMEM((rows, width), F32), pltpu.SemaphoreType.DMA((PIECES,)))

    block = jax.ShapeDtypeStruct((rows, width), BF16)
    x, y, both = call(prepare_kernel, (block, block, double), 1, (flags, images, texts))
    b1, a1 = move(x, first_x), move(y, first_y)
    b2, a2 = move(b1, later), move(a1, later)
    b3, a3 = move(b2, later), move(a2, later)
    mine = move(both, swap)
    step = rows
    other = [move(mine[at : at + step], cores) for at in range(0, 2 * rows, step)]

    acc, above, small = call(
        early_kernel,
        (totals, terms, terms),
        1,
        (scalars, tied(mine, a3), *other, a1, b1, a2, b2),
    )
    a4 = move(jnp.concatenate([a3, a2[:SPARE]]), later)
    (send_first,) = call(
        third_first_kernel, (wide,), 1, (scalars, *other[:2], a3, b3, acc, above, small)
    )
    back_first = move(send_first, home_first)
    acc, above, small = call(
        third_second_kernel,
        (total, term, term),
        1,
        (scalars, mine, tied(a3, send_first), b3, acc, above, small),
    )
    (send_second,) = call(fourth_kernel, (wide,), 1, (scalars, mine, a4, acc, above, small))
    send_second = tied(send_second, back_first)
    back_second = move(send_second, home_second)
    grad_images, grad_texts, loss = call(
        finish_first_kernel,
        (total, total, row),
        1,
        (flags, images, texts, tied(back_first, send_second)),
        outs_hbm=2,
        scratch=scratch,
    )
    grad_images, grad_texts, loss = call(
        finish_second_kernel,
        (total, total, row),
        1,
        (flags, images, texts, tied(back_second, loss), loss, grad_images, grad_texts),
        in_hbm=2,
        outs_hbm=2,
        scratch=scratch,
        aliases={5: 0, 6: 1},
    )
    return loss.reshape(rows), grad_images, grad_texts


def solution(mesh):
    return jax.shard_map(
        on_device,
        mesh=mesh,
        in_specs=(P(AXES, None), P(AXES, None), P(), P()),
        out_specs=(P(AXES), P(AXES, None), P(AXES, None)),
        check_vma=False,
    )
```
